32 devices in a mesh: blk: 8 (over z, x), inner: 4 (over y, core).
Axes of the slice: x: 2, y: 2, z: 4, core: 2. Of those that a mesh axis runs over, the one named last changes fastest.
Arguments:
- tokens: bfloat16 [4096, 4096], P(('blk', 'inner')), may hold values from -6 to 6
- expert_ids: int32 [4096, 8], P(('blk', 'inner')), may hold values from 0 to 15, all different within a row; in each aligned block of 128 rows (0 to 127, 128 to 255, ...) at most 96 rows name the same one
- route_weights: float32 [4096, 8], P(('blk', 'inner')), may hold values from 0.1 to 1
- w_in: bfloat16 [32, 4096, 768], P(('blk', 'inner')), may hold values from -0.09375 to 0.09375
- w_out: bfloat16 [32, 384, 4096], P(('blk', 'inner')), may hold values from -0.3125 to 0.3125
Outputs:
- moe_out: bfloat16 [4096, 4096], P(('blk', 'inner'))
The draws below stay inside these ranges and needn't reach their ends.
Inputs may be any that keep to these rules, and one draw needn't show every extreme that they name: `expert_ids`: each row names 8 different experts; among the 128 rows of one device no expert is named more than 96 times, a bound that some block reaches.
All inputs are finite; a program needn't handle non-finite values.
Results may differ from the reference program's by a relative error of at most 0.0085.
Values may be sent and summed in bfloat16 or wider, within the bound.
A program may use at most 128 MiB of HBM per device.

```python
import math
import jax
import jax.numpy as jnp
import numpy as np
from jax import lax

D = 4096
TOPK = 8
SPLIT = 2
STEPS = 3
TOK_DEV = 128
H_DEV = 384
EXP_GRP = 2
EXPERTS = 16
CAP = 96
TOKENS = 4096
N_BLK = 8
N_INNER = 4


def block_levels(stream_key, extent, cuts, low, high):
    loudness, own = 1.0, jax.random.fold_in(stream_key, 6)
    for position, parts in cuts:
        steps = jnp.exp(jax.random.uniform(jax.random.fold_in(own, position), (parts,), jnp.float32, low / len(cuts), high / len(cuts)))
        loudness = loudness * jnp.repeat(steps, extent[position] // parts).reshape([-1 if axis == position else 1 for axis in range(len(extent))])
    return loudness


def assign_block(rng, own, number, rows, number_of, top, limit, lean):
    order = jax.random.permutation(rng, number_of)
    heavy_load, common = portions_of(number_of, rows * top, limit, lean, True), portions_of(number_of, rows * top, limit, lean, False)
    places = jnp.arange(number_of)

    def named(lengths, turn):
        used = int((lengths > 0).sum())
        fixed = max(1, used // 4)
        shifted = fixed + (places - fixed + turn * (used - fixed)) % max(1, number_of - fixed)
        return jnp.zeros((number_of,), jnp.int32).at[order[jnp.where(places < fixed, places, shifted)]].set(jnp.asarray(lengths, jnp.int32))

    lengths = jnp.where(number % 4 == 0, named(heavy_load, number // 4), named(common, number - number // 4 - 1))
    mixed = jax.random.permutation(jax.random.fold_in(own, 3), number_of)
    source_of, receiver = mixed[0:number_of // 2 * 2:2], mixed[1:number_of // 2 * 2:2]
    slack = jnp.minimum(lengths[source_of] - 1, limit - lengths[receiver]) // 2
    slack = jnp.where((source_of == order[0]) | (receiver == order[0]) | (lengths[receiver] == 0), 0, jnp.maximum(slack, 0))
    shifted = jax.random.randint(jax.random.fold_in(own, 4), (number_of // 2,), 0, 1 << 20) % (slack + 1)
    lengths = lengths.at[source_of].add(-shifted).at[receiver].add(shifted)
    members = jnp.searchsorted(jnp.cumsum(lengths), jnp.arange(rows * top), side="right").astype(jnp.int32)
    grid = members.reshape(top, rows).T
    grid = grid[jax.random.permutation(jax.random.fold_in(own, 1), rows)]
    turn = jax.random.randint(jax.random.fold_in(own, 2), (rows, 1), 0, top)
    return jnp.take_along_axis(grid, (jnp.arange(top)[None, :] + turn) % top, axis=1)


def portions_of(count, total, limit, lean, full):
    loads = [(1 << 20) // math.isqrt(rank ** lean) + 1 for rank in range(1, count + 1)]
    largest = limit if full else min(limit, max(-(-total // count), total * loads[0] // sum(loads)))
    least = 1 if total - largest >= count - 1 else 0
    holding, surplus = [largest] + [least] * (count - 1), total - largest - least * (count - 1)
    while surplus > 0:
        free = [i for i in range(1, count) if holding[i] < largest] or [i for i in range(1, count) if holding[i] < limit]
        whole, remaining = sum([loads[i] for i in free]), surplus
        for i in free:
            extra = min(limit - holding[i], max(1, remaining * loads[i] // whole), surplus)
            holding[i] = holding[i] + extra
            surplus = surplus - extra
    return np.array(holding)


def scatter_about(stream_key, shape, scale, limit, pieces=(), held_as=jnp.bfloat16):
    array = scale * jax.random.normal(stream_key, shape, jnp.float32)
    if pieces:
        array = array * block_levels(stream_key, shape, pieces, -0.22, 0.18)
    return jnp.clip(array, -limit, limit).astype(held_as)


def setup_inputs(seed: int = 0) -> dict:
    seeds = jax.random.split(jax.random.key(seed), 6)
    tokens = scatter_about(seeds[0], (TOKENS, D), 1.0, 6.0, ((0, 32),))
    expert_ids_keys = jax.random.split(jax.random.fold_in(seeds[1], 1), TOKENS // TOK_DEV)
    expert_ids_turns = jax.random.permutation(jax.random.fold_in(seeds[1], 3), TOKENS // TOK_DEV)
    expert_ids = jax.vmap(lambda own, number: assign_block(jax.random.fold_in(seeds[1], 2), own, number, TOK_DEV, EXPERTS, TOPK, CAP, 2))(expert_ids_keys, expert_ids_turns).reshape((TOKENS, TOPK))
    route_weights = jnp.clip(jnp.exp(math.log(1.0) - 2.3025851 * jax.random.uniform(seeds[2], (TOKENS, TOPK), jnp.float32) ** block_levels(seeds[2], (TOKENS, TOPK), ((0, 32),), -0.2, 0.2)), 0.1, 1.0)
    w_in = scatter_about(seeds[3], (EXPERTS * SPLIT, D, 2 * H_DEV), D ** -0.5, 0.09375, ((0, 32),))
    w_out = scatter_about(seeds[4], (EXPERTS * SPLIT, H_DEV, D), H_DEV ** -0.5, 0.3125, ((0, 32),))
    return {"tokens": tokens, "expert_ids": expert_ids, "route_weights": route_weights, "w_in": w_in, "w_out": w_out}


def reference(tokens, expert_ids, route_weights, w_in, w_out):
    group_of = jnp.arange(TOKENS, dtype=jnp.int32) // (N_INNER * TOK_DEV)
    home_group = expert_ids // EXP_GRP
    counted = jnp.mod(group_of[:, None] - home_group, N_BLK) < STEPS
    max_rows = STEPS * N_INNER * CAP

    def one_expert(accumulated, expert):
        member = counted & (expert_ids == expert)
        weight = jnp.sum(jnp.where(member, route_weights, jnp.zeros_like(route_weights)), axis=1)
        chosen = jnp.any(member, axis=1)
        row_count = jnp.sum(chosen.astype(jnp.int32))
        row_index = jnp.nonzero(chosen, size=max_rows, fill_value=0)[0].astype(jnp.int32)
        live_rows = jnp.arange(max_rows, dtype=jnp.int32) < row_count
        row_scale = jnp.where(live_rows, weight[row_index], jnp.zeros_like(weight[row_index]))
        gathered = tokens[row_index]
        mixture = jnp.zeros((max_rows, D), jnp.float32)
        for half_index in range(SPLIT):
            slice_index = expert * SPLIT + half_index
            projected = jnp.dot(gathered, w_in[slice_index], preferred_element_type=jnp.float32)
            activated = (jax.nn.silu(projected[:, :H_DEV]) * projected[:, H_DEV:]).astype(jnp.bfloat16)
            partial_value = jnp.dot(activated, w_out[slice_index], preferred_element_type=jnp.float32).astype(jnp.bfloat16)
            partial_value = lax.optimization_barrier(partial_value)
            mixture = mixture + partial_value.astype(jnp.float32)
        accumulated = accumulated.at[row_index].add(row_scale[:, None] * mixture)
        return accumulated, None

    accumulated, _ = lax.scan(one_expert, jnp.zeros((TOKENS, D), jnp.float32), jnp.arange(EXPERTS, dtype=jnp.int32))
    return accumulated.astype(jnp.bfloat16)
```

```python
import jax
import jax.numpy as jnp
from jax import lax
from jax.experimental import pallas as pl
from jax.experimental.pallas import tpu as pltpu
from jax.sharding import PartitionSpec as P

SPLIT = 2
STEPS = 3
CHUNKS = 4
MESH = pl.DeviceIdType.MESH


def passed_along(value, axis, steps):
    count = lax.axis_size(axis)
    pairs = [(source, (source + steps) % count) for source in range(count)]
    return lax.ppermute(value, axis, pairs)


def on_device_general(tokens, expert_ids, route_weights, w_in, w_out):
    inner_count = lax.axis_size("inner")
    blk_count = lax.axis_size("blk")
    hidden = w_out.shape[1]
    gathered, ids, scales = (
        lax.all_gather(v, "inner", axis=0, tiled=True) for v in (tokens, expert_ids, route_weights)
    )
    current = (w_in, w_out)
    result = jnp.zeros(gathered.shape, jnp.float32)
    for rotation in range(STEPS):
        home = jnp.mod(lax.axis_index("blk") - rotation, blk_count)
        expert = home * (inner_count // SPLIT) + lax.axis_index("inner") // SPLIT
        if rotation > 0:
            current = passed_along(current, "blk", 1)
        scale = jnp.sum(jnp.where(ids == expert, scales, 0.0), axis=1, keepdims=True)
        projected = jnp.dot(gathered, current[0][0], preferred_element_type=jnp.float32)
        activated = (jax.nn.silu(projected[:, :hidden]) * projected[:, hidden:]).astype(jnp.bfloat16)
        partial = jnp.dot(activated, current[1][0], preferred_element_type=jnp.float32)
        result = result + scale * partial
    return lax.psum_scatter(
        result.astype(jnp.bfloat16), "inner", scatter_dimension=0, tiled=True
    ).astype(jnp.bfloat16)


def moe_kernel(
    tok_ref, aux_ref, w_in_ref, w_out_ref, out_ref,
    x_ref, aux_all, w_in_vm, w_out_vm, proj, act,
    own, sib_out, sib_in, from_x, from_y, from_z,
    local_sem, xs, xr, us, ur, qs, qr, a_s, a_r, b_s, b_r, z_s, z_r,
):
    blk = lax.axis_size("blk")
    h, i = lax.axis_index("blk"), lax.axis_index("inner")
    tok = tok_ref.shape[0]
    rows = tok // CHUNKS
    hidden = w_out_vm.shape[0]
    model = w_out_vm.shape[1]
    x = lax.rem(h, 2)
    y, k = i // 2, lax.rem(i, 2)
    r_of_x = 2 * (1 - x)
    sib = (h, 2 * y + 1 - k)
    y_dev = (h, 2 * (1 - y) + k)
    x_dev = (h + 1 - 2 * x, i)
    z_down = (lax.rem(h + blk - 2, blk), i)
    z_up = (lax.rem(h + 2, blk), i)

    def part(c):
        return pl.ds(c * rows, rows)

    def slot_rows(dk, c):
        return pl.ds(dk * tok + c * rows, rows)

    def remote(src, dst, s, r, device):
        return pltpu.make_async_remote_copy(
            src_ref=src, dst_ref=dst, send_sem=s, recv_sem=r, device_id=device, device_id_type=MESH
        )

    def x_copy(slot, c, src, device):
        r, dy, dk = slot
        at = (r * 2 + dy) * 2 + dk
        return remote(
            src, x_ref.at[r, dy, slot_rows(dk, c), :], xs.at[at, c], xr.at[at, c], device
        )

    def held(r, dy, c):
        return x_ref.at[r, dy, slot_rows(0, c), :]

    def got(slot, c):
        x_copy(slot, c, held(0, 0, c), sib).wait_recv()

    def aux_copy(r, dy, dk):
        at = (r * 2 + dy) * 2 + dk
        y_to = y if dy == 0 else 1 - y
        k_to = k if dk == 0 else 1 - k
        device = (lax.rem(h + blk - r, blk), 2 * y_to + k_to)
        return remote(aux_ref, aux_all.at[r, dy, dk], us.at[at], ur.at[at], device)

    def q_copy(r, dy):
        at = r * 2 + dy
        return remote(sib_out.at[r, dy], sib_in.at[r, dy], qs.at[at], qr.at[at], sib)

    def a_copy(dy, c):
        return remote(
            own.at[1, dy, part(c), :], from_x.at[dy, part(c), :], a_s.at[dy, c], a_r.at[dy, c], x_dev
        )

    def b_copy(half, c):
        return remote(
            own.at[2 * half, 1, part(c), :], from_y.at[half, part(c), :],
            b_s.at[half, c], b_r.at[half, c], y_dev,
        )

    def z_copy(c):
        return remote(own.at[2, 0, part(c), :], from_z.at[part(c), :], z_s.at[c], z_r.at[c], z_up)

    loads = [
        pltpu.make_async_copy(tok_ref, x_ref.at[0, 0, pl.ds(0, tok), :], local_sem.at[0]),
        pltpu.make_async_copy(w_in_ref.at[0], w_in_vm, local_sem.at[1]),
        pltpu.make_async_copy(w_out_ref.at[0], w_out_vm, local_sem.at[2]),
    ]
    for load in loads:
        load.start()

    barrier = pltpu.get_barrier_semaphore()
    peers = 0
    for r in range(-2, 3):
        for dy in range(2):
            for dk in range(2):
                if (r, dy, dk) == (0, 0, 0):
                    continue
                y_to = y if dy == 0 else 1 - y
                k_to = k if dk == 0 else 1 - k
                pl.semaphore_signal(
                    barrier, inc=1,
                    device_id=(lax.rem(h + blk + r, blk), 2 * y_to + k_to), device_id_type=MESH,
                )
                peers += 1
    pl.semaphore_wait(barrier, peers)

    for c in range(CHUNKS):
        mine = tok_ref.at[part(c), :]
        x_copy((2, 0, 0), c, mine, z_down).start()
        x_copy((0, 1, 0), c, mine, y_dev).start()

        @pl.when(x == 1)
        def _():
            x_copy((1, 0, 0), c, mine, x_dev).start()

        x_copy((0, 0, 1), c, mine, sib).start()
    slots = [(r, dy, dk) for r in range(3) for dy in range(2) for dk in range(2)][1:]
    for slot in slots:
        aux_copy(*slot).start()
    aux_all[0, 0, 0] = aux_ref[...]

    expert = 2 * h + y

    def scale_of(r, dy, dk):
        table = aux_all[r, dy, dk]
        line = jnp.sum(
            jnp.where(lax.broadcasted_iota(jnp.int32, table.shape, 0) == expert, table, 0.0),
            axis=0, keepdims=True,
        )
        square = (tok, tok)
        same = lax.broadcasted_iota(jnp.int32, square, 0) == lax.broadcasted_iota(jnp.int32, square, 1)
        return jnp.sum(
            jnp.where(same, jnp.broadcast_to(line, square), 0.0), axis=1, keepdims=True
        )

    def compute(r, dy):
        for dk in range(2):
            if (r, dy, dk) != (0, 0, 0):
                aux_copy(r, dy, dk).wait_recv()
        for c in range(CHUNKS):
            got((r, dy, 1), c)

        def in_step(n, carry):
            cols = pl.ds(pl.multiple_of(n * 256, 256), 256)
            proj[:, cols] = jnp.dot(x_ref[r, dy], w_in_vm[:, cols], preferred_element_type=jnp.float32)
            return carry

        lax.fori_loop(0, 2 * hidden // 256, in_step, 0)
        for dk in range(2):
            line = pl.ds(dk * tok, tok)
            gate = proj[line, pl.ds(0, hidden)]
            up = proj[line, pl.ds(hidden, hidden)]
            act[line, :] = (gate / (1.0 + jnp.exp(-gate)) * up * scale_of(r, dy, dk)).astype(
                jnp.bfloat16
            )

        def out_step(n, carry):
            cols = pl.ds(pl.multiple_of(n * 512, 512), 512)
            value = jnp.dot(act[...], w_out_vm[:, cols], preferred_element_type=jnp.float32)
            own[r, dy, :, cols] = value[:tok].astype(jnp.bfloat16)
            sib_out[r, dy, :, cols] = value[tok:].astype(jnp.bfloat16)
            return carry

        lax.fori_loop(0, model // 512, out_step, 0)
        q_copy(r, dy).start()

    def add_up(r, dy, c, *more):
        total = own[r, dy, part(c), :].astype(jnp.float32)
        total = total + sib_in[r, dy, part(c), :].astype(jnp.float32)
        for term in more:
            total = total + term.astype(jnp.float32)
        return total

    for load in loads:
        load.wait()
    compute(0, 0)
    for c in range(CHUNKS):
        got((2, 0, 0), c)

        @pl.when(x == 0)
        def _():
            x_copy((1, 0, 0), c, held(2, 0, c), x_dev).start()

        x_copy((2, 1, 0), c, held(2, 0, c), y_dev).start()
        x_copy((2, 0, 1), c, held(2, 0, c), sib).start()
        got((0, 1, 0), c)

        @pl.when(x == 1)
        def _():
            x_copy((1, 1, 0), c, held(0, 1, c), x_dev).start()

        x_copy((0, 1, 1), c, held(0, 1, c), sib).start()
    compute(0, 1)
    compute(2, 0)
    for c in range(CHUNKS):
        got((1, 0, 0), c)
        x_copy((1, 0, 1), c, held(1, 0, c), sib).start()
        got((2, 1, 0), c)

        @pl.when(x == 0)
        def _():
            x_copy((1, 1, 0), c, held(2, 1, c), x_dev).start()

        x_copy((2, 1, 1), c, held(2, 1, c), sib).start()
    compute(1, 0)
    compute(2, 1)
    q_copy(1, 0).wait_recv()
    for c in range(CHUNKS):
        own[1, 0, part(c), :] = add_up(1, 0, c).astype(jnp.bfloat16)
        a_copy(0, c).start()
    q_copy(0, 1).wait_recv()
    q_copy(2, 1).wait_recv()
    r_plain = 2 - r_of_x
    for c in range(CHUNKS):
        own[r_plain, 1, part(c), :] = add_up(r_plain, 1, c).astype(jnp.bfloat16)
        b_copy(r_plain // 2, c).start()
    for c in range(CHUNKS):
        got((1, 1, 0), c)
        x_copy((1, 1, 1), c, held(1, 1, c), sib).start()
    compute(1, 1)
    q_copy(1, 1).wait_recv()
    for c in range(CHUNKS):
        own[1, 1, part(c), :] = add_up(1, 1, c).astype(jnp.bfloat16)
        a_copy(1, c).start()
    q_copy(0, 0).wait_recv()
    q_copy(2, 0).wait_recv()
    for c in range(CHUNKS):
        a_copy(0, c).wait_recv()
        own[r_of_x, 0, part(c), :] = add_up(r_of_x, 0, c, from_x[0, part(c), :]).astype(jnp.bfloat16)
        own[r_plain, 0, part(c), :] = add_up(r_plain, 0, c).astype(jnp.bfloat16)
    for c in range(CHUNKS):
        a_copy(1, c).wait_recv()
        own[r_of_x, 1, part(c), :] = add_up(r_of_x, 1, c, from_x[1, part(c), :]).astype(jnp.bfloat16)
        b_copy(r_of_x // 2, c).start()
    for c in range(CHUNKS):
        b_copy(1, c).wait_recv()
        own[2, 0, part(c), :] = (
            own[2, 0, part(c), :].astype(jnp.float32) + from_y[1, part(c), :].astype(jnp.float32)
        ).astype(jnp.bfloat16)
        z_copy(c).start()
    for c in range(CHUNKS):
        b_copy(0, c).wait_recv()
        z_copy(c).wait_recv()
        out_ref[part(c), :] = (
            own[0, 0, part(c), :].astype(jnp.float32)
            + from_y[0, part(c), :].astype(jnp.float32)
            + from_z[part(c), :].astype(jnp.float32)
        ).astype(jnp.bfloat16)

    for slot in slots:
        aux_copy(*slot).wait_send()
        for c in range(CHUNKS):
            x_copy(slot, c, held(0, 0, c), sib).wait_send()
    for r in range(3):
        for dy in range(2):
            q_copy(r, dy).wait_send()
    for c in range(CHUNKS):
        for half in range(2):
            a_copy(half, c).wait_send()
            b_copy(half, c).wait_send()
        z_copy(c).wait_send()


def on_device_kernel(tokens, expert_ids, route_weights, w_in, w_out):
    tok, model = tokens.shape
    hidden = w_out.shape[1]
    experts = lax.axis_size("inner") // SPLIT * lax.axis_size("blk")
    matches = expert_ids.T[None, :, :] == jnp.arange(experts, dtype=jnp.int32)[:, None, None]
    table = jnp.sum(jnp.where(matches, route_weights.T[None, :, :], 0.0), axis=1)
    hbm = pl.BlockSpec(memory_space=pl.ANY)
    vmem = pl.BlockSpec(memory_space=pltpu.VMEM)
    dma = pltpu.SemaphoreType.DMA
    bf16 = jnp.bfloat16
    return pl.pallas_call(
        moe_kernel,
        out_shape=jax.ShapeDtypeStruct((tok, model), bf16),
        in_specs=[hbm, vmem, hbm, hbm],
        out_specs=vmem,
        scratch_shapes=[
            pltpu.VMEM((3, 2, 2 * tok, model), bf16),
            pltpu.VMEM((3, 2, 2, experts, tok), jnp.float32),
            pltpu.VMEM(w_in.shape[1:], bf16),
            pltpu.VMEM(w_out.shape[1:], bf16),
            pltpu.VMEM((2 * tok, 2 * hidden), jnp.float32),
            pltpu.VMEM((2 * tok, hidden), bf16),
            pltpu.VMEM((3, 2, tok, model), bf16),
            pltpu.VMEM((3, 2, tok, model), bf16),
            pltpu.VMEM((3, 2, tok, model), bf16),
            pltpu.VMEM((2, tok, model), bf16),
            pltpu.VMEM((2, tok, model), bf16),
            pltpu.VMEM((tok, model), bf16),
            dma((3,)),
            dma((12, CHUNKS)),
            dma((12, CHUNKS)),
            dma((12,)),
            dma((12,)),
            dma((6,)),
            dma((6,)),
            dma((2, CHUNKS)),
            dma((2, CHUNKS)),
            dma((2, CHUNKS)),
            dma((2, CHUNKS)),
            dma((CHUNKS,)),
            dma((CHUNKS,)),
        ],
        compiler_params=pltpu.CompilerParams(
            collective_id=0, has_side_effects=True, vmem_limit_bytes=58 * 1024 * 1024
        ),
    )(tokens, table, w_in, w_out)


def solution(mesh):
    small = mesh.shape["inner"] == 4 and mesh.shape["blk"] % 2 == 0 and mesh.shape["blk"] >= 6
    on_device = on_device_kernel if small else on_device_general
    return jax.shard_map(
        on_device,
        mesh=mesh,
        in_specs=(
            P(("blk", "inner"), None),
            P(("blk", "inner"), None),
            P(("blk", "inner"), None),
            P(("blk", "inner"), None, None),
            P(("blk", "inner"), None, None),
        ),
        out_specs=P(("blk", "inner"), None),
        check_vma=False,
    )
```

```python
import jax
import jax.numpy as jnp
from jax import lax
from jax.experimental import pallas as pl
from jax.experimental.pallas import tpu as pltpu
from jax.sharding import PartitionSpec as P

SPLIT = 2
STEPS = 3
CHUNKS = 4
EARLY = (0, 1)
LATE = (2, 3)
MESH = pl.DeviceIdType.MESH


def passed_along(value, axis, steps):
    count = lax.axis_size(axis)
    pairs = [(source, (source + steps) % count) for source in range(count)]
    return lax.ppermute(value, axis, pairs)


def on_device_general(tokens, expert_ids, route_weights, w_in, w_out):
    inner_count = lax.axis_size("inner")
    blk_count = lax.axis_size("blk")
    hidden = w_out.shape[1]
    gathered, ids, scales = (
        lax.all_gather(v, "inner", axis=0, tiled=True) for v in (tokens, expert_ids, route_weights)
    )
    current = (w_in, w_out)
    result = jnp.zeros(gathered.shape, jnp.float32)
    for rotation in range(STEPS):
        home = jnp.mod(lax.axis_index("blk") - rotation, blk_count)
        expert = home * (inner_count // SPLIT) + lax.axis_index("inner") // SPLIT
        if rotation > 0:
            current = passed_along(current, "blk", 1)
        scale = jnp.sum(jnp.where(ids == expert, scales, 0.0), axis=1, keepdims=True)
        projected = jnp.dot(gathered, current[0][0], preferred_element_type=jnp.float32)
        activated = (jax.nn.silu(projected[:, :hidden]) * projected[:, hidden:]).astype(jnp.bfloat16)
        partial = jnp.dot(activated, current[1][0], preferred_element_type=jnp.float32)
        result = result + scale * partial
    return lax.psum_scatter(
        result.astype(jnp.bfloat16), "inner", scatter_dimension=0, tiled=True
    ).astype(jnp.bfloat16)


def moe_kernel(
    tok_ref, aux_ref, w_in_ref, w_out_ref, out_ref,
    x_ref, aux_all, w_in_vm, w_out_vm, proj, act,
    own, sib_out, sib_in, from_x, from_y, from_z,
    local_sem, xs, xr, us, ur, qs, qr, a_s, a_r, b_s, b_r, z_s, z_r,
):
    blk = lax.axis_size("blk")
    h, i = lax.axis_index("blk"), lax.axis_index("inner")
    tok = tok_ref.shape[0]
    rows = tok // CHUNKS
    hidden = w_out_vm.shape[0]
    model = w_out_vm.shape[1]
    x = lax.rem(h, 2)
    y, k = i // 2, lax.rem(i, 2)
    sib = (h, 2 * y + 1 - k)
    y_dev = (h, 2 * (1 - y) + k)
    x_dev = (h + 1 - 2 * x, i)
    z_down = (lax.rem(h + blk - 2, blk), i)
    z_up = (lax.rem(h + 2, blk), i)

    def part(c):
        return pl.ds(c * rows, rows)

    def slot_rows(dk, c):
        return pl.ds(dk * tok + c * rows, rows)

    def remote(src, dst, s, r, device):
        return pltpu.make_async_remote_copy(
            src_ref=src, dst_ref=dst, send_sem=s, recv_sem=r, device_id=device, device_id_type=MESH
        )

    def x_copy(slot, c, src, device):
        r, dy, dk = slot
        at = (r * 2 + dy) * 2 + dk
        return remote(
            src, x_ref.at[r, dy, slot_rows(dk, c), :], xs.at[at, c], xr.at[at, c], device
        )

    def held(r, dy, c):
        return x_ref.at[r, dy, slot_rows(0, c), :]

    def got(slot, c):
        x_copy(slot, c, held(0, 0, c), sib).wait_recv()

    def aux_copy(r, dy, dk):
        at = (r * 2 + dy) * 2 + dk
        y_to = y if dy == 0 else 1 - y
        k_to = k if dk == 0 else 1 - k
        device = (lax.rem(h + blk - r, blk), 2 * y_to + k_to)
        return remote(aux_ref, aux_all.at[r, dy, dk], us.at[at], ur.at[at], device)

    def q_copy(r, dy):
        at = r * 2 + dy
        return remote(sib_out.at[r, dy], sib_in.at[r, dy], qs.at[at], qr.at[at], sib)

    def a_copy(dy, c):
        return remote(
            own.at[1, dy, part(c), :], from_x.at[dy, part(c), :], a_s.at[dy, c], a_r.at[dy, c], x_dev
        )

    def b_copy(r, c):
        return remote(
            own.at[r, 1, part(c), :], from_y.at[r, part(c), :], b_s.at[r, c], b_r.at[r, c], y_dev
        )

    def z_copy(dy, c):
        return remote(
            own.at[2, dy, part(c), :], from_z.at[dy, part(c), :], z_s.at[dy, c], z_r.at[dy, c], z_up
        )

    loads = [
        pltpu.make_async_copy(tok_ref, x_ref.at[0, 0, pl.ds(0, tok), :], local_sem.at[0]),
        pltpu.make_async_copy(w_in_ref.at[0], w_in_vm, local_sem.at[1]),
        pltpu.make_async_copy(w_out_ref.at[0], w_out_vm, local_sem.at[2]),
    ]
    for load in loads:
        load.start()

    barrier = pltpu.get_barrier_semaphore()
    peers = 0
    for r in range(-2, 3):
        for dy in range(2):
            for dk in range(2):
                if (r, dy, dk) == (0, 0, 0):
                    continue
                y_to = y if dy == 0 else 1 - y
                k_to = k if dk == 0 else 1 - k
                pl.semaphore_signal(
                    barrier, inc=1,
                    device_id=(lax.rem(h + blk + r, blk), 2 * y_to + k_to), device_id_type=MESH,
                )
                peers += 1
    pl.semaphore_wait(barrier, peers)

    for c in range(CHUNKS):
        mine = tok_ref.at[part(c), :]
        x_copy((2, 0, 0), c, mine, z_down).start()
        x_copy((0, 1, 0), c, mine, y_dev).start()

        @pl.when(x == 1)
        def _():
            x_copy((1, 0, 0), c, mine, x_dev).start()

        x_copy((0, 0, 1), c, mine, sib).start()
    slots = [(r, dy, dk) for r in range(3) for dy in range(2) for dk in range(2)][1:]
    for slot in slots:
        aux_copy(*slot).start()
    aux_all[0, 0, 0] = aux_ref[...]

    expert = 2 * h + y

    def scale_of(r, dy, dk):
        table = aux_all[r, dy, dk]
        line = jnp.sum(
            jnp.where(lax.broadcasted_iota(jnp.int32, table.shape, 0) == expert, table, 0.0),
            axis=0, keepdims=True,
        )
        square = (tok, tok)
        same = lax.broadcasted_iota(jnp.int32, square, 0) == lax.broadcasted_iota(jnp.int32, square, 1)
        return jnp.sum(
            jnp.where(same, jnp.broadcast_to(line, square), 0.0), axis=1, keepdims=True
        )

    def compute(r, dy):
        for dk in range(2):
            if (r, dy, dk) != (0, 0, 0):
                aux_copy(r, dy, dk).wait_recv()
        for c in range(CHUNKS):
            got((r, dy, 1), c)

        def in_step(n, carry):
            cols = pl.ds(pl.multiple_of(n * 256, 256), 256)
            proj[:, cols] = jnp.dot(x_ref[r, dy], w_in_vm[:, cols], preferred_element_type=jnp.float32)
            return carry

        lax.fori_loop(0, 2 * hidden // 256, in_step, 0)
        for dk in range(2):
            line = pl.ds(dk * tok, tok)
            gate = proj[line, pl.ds(0, hidden)]
            up = proj[line, pl.ds(hidden, hidden)]
            act[line, :] = (gate / (1.0 + jnp.exp(-gate)) * up * scale_of(r, dy, dk)).astype(
                jnp.bfloat16
            )

        def out_step(n, carry):
            cols = pl.ds(pl.multiple_of(n * 512, 512), 512)
            value = jnp.dot(act[...], w_out_vm[:, cols], preferred_element_type=jnp.float32)
            own[r, dy, :, cols] = value[:tok].astype(jnp.bfloat16)
            sib_out[r, dy, :, cols] = value[tok:].astype(jnp.bfloat16)
            return carry

        lax.fori_loop(0, model // 512, out_step, 0)
        q_copy(r, dy).start()

    def add_up(r, dy, c, *more):
        total = own[r, dy, part(c), :].astype(jnp.float32)
        total = total + sib_in[r, dy, part(c), :].astype(jnp.float32)
        for term in more:
            total = total + term[part(c), :].astype(jnp.float32)
        return total.astype(jnp.bfloat16)

    def settle(r, dy, c, *more):
        own[r, dy, part(c), :] = add_up(r, dy, c, *more)

    def spread_near(c):
        got((1, 0, 0), c)
        if c in LATE:
            x_copy((1, 1, 0), c, held(1, 0, c), y_dev).start()
        x_copy((1, 0, 1), c, held(1, 0, c), sib).start()

    def spread_far(c):
        got((2, 1, 0), c)
        if c in EARLY:

            @pl.when(x == 0)
            def _():
                x_copy((1, 1, 0), c, held(2, 1, c), x_dev).start()

        x_copy((2, 1, 1), c, held(2, 1, c), sib).start()

    for load in loads:
        load.wait()
    compute(0, 0)
    for c in range(CHUNKS):
        got((2, 0, 0), c)

        @pl.when(x == 0)
        def _():
            x_copy((1, 0, 0), c, held(2, 0, c), x_dev).start()

        if c in LATE:
            x_copy((2, 1, 0), c, held(2, 0, c), y_dev).start()
        x_copy((2, 0, 1), c, held(2, 0, c), sib).start()
        got((0, 1, 0), c)
        if c in EARLY:
            x_copy((2, 1, 0), c, held(0, 1, c), z_down).start()

            @pl.when(x == 1)
            def _():
                x_copy((1, 1, 0), c, held(0, 1, c), x_dev).start()

        x_copy((0, 1, 1), c, held(0, 1, c), sib).start()
        if c > 0:
            spread_near(c - 1)
    spread_near(CHUNKS - 1)
    compute(1, 0)
    spread_far(0)
    compute(2, 0)
    q_copy(1, 0).wait_recv()
    for c in EARLY:
        settle(1, 0, c)
        a_copy(0, c).start()
    for c in range(1, CHUNKS):
        spread_far(c)
    q_copy(2, 0).wait_recv()

    @pl.when(x == 1)
    def _():
        for c in EARLY:
            settle(2, 0, c)
            z_copy(0, c).start()

    compute(2, 1)
    for c in range(CHUNKS):
        got((1, 1, 0), c)
        x_copy((1, 1, 1), c, held(1, 1, c), sib).start()
    q_copy(2, 1).wait_recv()
    for c in LATE:
        settle(2, 1, c)
        b_copy(2, c).start()

    @pl.when(x == 1)
    def _():
        for c in EARLY:
            settle(2, 1, c)
            z_copy(1, c).start()

    compute(1, 1)
    q_copy(1, 1).wait_recv()
    for c in LATE:
        settle(1, 1, c)
        b_copy(1, c).start()
    for c in EARLY:
        settle(1, 1, c)
        a_copy(1, c).start()

    @pl.when(x == 0)
    def _():
        for c in EARLY:
            a_copy(0, c).wait_recv()
            settle(2, 0, c, from_x.at[0])
            z_copy(0, c).start()

    compute(0, 1)
    for c in LATE:
        b_copy(1, c).wait_recv()
        settle(1, 0, c, from_y.at[1])
        a_copy(0, c).start()
    q_copy(0, 1).wait_recv()
    for c in LATE:
        settle(0, 1, c)
        b_copy(0, c).start()

    @pl.when(x == 0)
    def _():
        for c in EARLY:
            a_copy(1, c).wait_recv()
            settle(2, 1, c, from_x.at[1])
            z_copy(1, c).start()

    for c in LATE:
        b_copy(2, c).wait_recv()

        @pl.when(x == 0)
        def _():
            a_copy(0, c).wait_recv()
            settle(2, 0, c, from_y.at[2], from_x.at[0])

        @pl.when(x == 1)
        def _():
            settle(2, 0, c, from_y.at[2])

        z_copy(0, c).start()
    for c in EARLY:
        z_copy(1, c).wait_recv()

        @pl.when(x == 0)
        def _():
            settle(0, 1, c, from_z.at[1])

        @pl.when(x == 1)
        def _():
            a_copy(1, c).wait_recv()
            settle(0, 1, c, from_z.at[1], from_x.at[1])

        b_copy(0, c).start()
    q_copy(0, 0).wait_recv()
    for c in range(CHUNKS):
        z_copy(0, c).wait_recv()
        b_copy(0, c).wait_recv()

        @pl.when(x == 0)
        def _():
            out_ref[part(c), :] = add_up(0, 0, c, from_z.at[0], from_y.at[0])

        @pl.when(x == 1)
        def _():
            a_copy(0, c).wait_recv()
            out_ref[part(c), :] = add_up(0, 0, c, from_z.at[0], from_y.at[0], from_x.at[0])

    for slot in slots:
        aux_copy(*slot).wait_send()
        for c in range(CHUNKS):
            x_copy(slot, c, held(0, 0, c), sib).wait_send()
    for r in range(3):
        for dy in range(2):
            q_copy(r, dy).wait_send()
    for c in range(CHUNKS):
        a_copy(0, c).wait_send()
        b_copy(0, c).wait_send()
        z_copy(0, c).wait_send()
        if c in EARLY:
            a_copy(1, c).wait_send()
            z_copy(1, c).wait_send()
        else:
            b_copy(1, c).wait_send()
            b_copy(2, c).wait_send()


def on_device_kernel(tokens, expert_ids, route_weights, w_in, w_out):
    tok, model = tokens.shape
    hidden = w_out.shape[1]
    experts = lax.axis_size("inner") // SPLIT * lax.axis_size("blk")
    matches = expert_ids.T[None, :, :] == jnp.arange(experts, dtype=jnp.int32)[:, None, None]
    table = jnp.sum(jnp.where(matches, route_weights.T[None, :, :], 0.0), axis=1)
    hbm = pl.BlockSpec(memory_space=pl.ANY)
    vmem = pl.BlockSpec(memory_space=pltpu.VMEM)
    dma = pltpu.SemaphoreType.DMA
    bf16 = jnp.bfloat16
    return pl.pallas_call(
        moe_kernel,
        out_shape=jax.ShapeDtypeStruct((tok, model), bf16),
        in_specs=[hbm, vmem, hbm, hbm],
        out_specs=vmem,
        scratch_shapes=[
            pltpu.VMEM((3, 2, 2 * tok, model), bf16),
            pltpu.VMEM((3, 2, 2, experts, tok), jnp.float32),
            pltpu.VMEM(w_in.shape[1:], bf16),
            pltpu.VMEM(w_out.shape[1:], bf16),
            pltpu.VMEM((2 * tok, 2 * hidden), jnp.float32),
            pltpu.VMEM((2 * tok, hidden), bf16),
            pltpu.VMEM((3, 2, tok, model), bf16),
            pltpu.VMEM((3, 2, tok, model), bf16),
            pltpu.VMEM((3, 2, tok, model), bf16),
            pltpu.VMEM((2, tok, model), bf16),
            pltpu.VMEM((3, tok, model), bf16),
            pltpu.VMEM((2, tok, model), bf16),
            dma((3,)),
            dma((12, CHUNKS)),
            dma((12, CHUNKS)),
            dma((12,)),
            dma((12,)),
            dma((6,)),
            dma((6,)),
            dma((2, CHUNKS)),
            dma((2, CHUNKS)),
            dma((3, CHUNKS)),
            dma((3, CHUNKS)),
            dma((2, CHUNKS)),
            dma((2, CHUNKS)),
        ],
        compiler_params=pltpu.CompilerParams(
            collective_id=0, has_side_effects=True, vmem_limit_bytes=58 * 1024 * 1024
        ),
    )(tokens, table, w_in, w_out)


def solution(mesh):
    small = mesh.shape["inner"] == 4 and mesh.shape["blk"] % 2 == 0 and mesh.shape["blk"] >= 6
    on_device = on_device_kernel if small else on_device_general
    return jax.shard_map(
        on_device,
        mesh=mesh,
        in_specs=(
            P(("blk", "inner"), None),
            P(("blk", "inner"), None),
            P(("blk", "inner"), None),
            P(("blk", "inner"), None, None),
            P(("blk", "inner"), None, None),
        ),
        out_specs=P(("blk", "inner"), None),
        check_vma=False,
    )
```
